128 devices in a mesh: blk: 32 (over z, x, y_hi), rep: 4 (over y_lo, core).
Axes of the slice: x: 4, y: 4 (y_hi: 2, y_lo: 2; y = y_hi * 2 + y_lo), z: 4, core: 2. Of those that a mesh axis runs over, the one named last changes fastest.
Arguments:
- img_feat: bfloat16 [8192, 1152], P('blk'), may hold values from -6 to 6
- txt_feat: bfloat16 [8192, 1152], P('blk'), may hold values from -6 to 6
- img_weight: bfloat16 [1152, 1152], replicated, may hold values from -0.1875 to 0.1875
- txt_weight: bfloat16 [1152, 1152], replicated, may hold values from -0.1875 to 0.1875
- logit_scale: float32 [1], replicated, may hold values from 5 to 20
- logit_bias: float32 [1], replicated, may hold values from -2 to 0
Outputs:
- grad_img_feat: bfloat16 [8192, 1152], P(('blk', 'rep'))
- grad_txt_feat: bfloat16 [8192, 1152], P(('blk', 'rep'))
- grad_img_weight: float32 [1152, 1152], P(('blk', 'rep'))
- grad_txt_weight: float32 [1152, 1152], P(('blk', 'rep'))
The draws below stay inside these ranges and needn't reach their ends.
All inputs are finite; a program needn't handle non-finite values.
Results may differ from the reference program's by a relative error of at most 0.02.
Values may be sent and summed in bfloat16 or wider, within the bound.
A program may use at most 128 MiB of HBM per device.

```python
import math
import jax
import jax.numpy as jnp
from jax import lax

D = 1152
PAIRS = 8192


def strengthened(entries, stream_key, source, target, parts, factor):
    owner, partner = [(jnp.arange(entries.shape[axis_at]) // (entries.shape[axis_at] // parts)).reshape([-1 if axis == axis_at else 1 for axis in range(entries.ndim)]) for axis_at in (source, target)]
    chosen = jax.random.permutation(stream_key, parts)[partner]
    strong = (owner == chosen) | (owner == (partner + parts // 2) % parts)
    return jnp.where(strong, factor * entries, entries)


def shard_levels(stream_key, extent, split, low, high):
    gain = 1.0
    for position, shards_of in split:
        draws = jax.random.uniform(jax.random.fold_in(jax.random.fold_in(stream_key, 6), position), (shards_of,), jnp.float32, low / len(split), high / len(split))
        gain = gain * jnp.repeat(jnp.exp(draws), extent[position] // shards_of).reshape((-1,) + (1,) * (len(extent) - 1 - position))
    return gain


def scatter_about(stream_key, dims, width, bound, split=(), kind=jnp.bfloat16):
    result = width * jax.random.normal(stream_key, dims, jnp.float32)
    if split:
        result = result * shard_levels(stream_key, dims, split, -0.22, 0.18)
    return jnp.clip(result, -bound, bound).astype(kind)


def gaussian_with(rng, dims, spread, reach, shards, heavy, kind=jnp.bfloat16):
    values = spread * jax.random.normal(rng, dims, jnp.float32)
    if shards:
        values = values * shard_levels(rng, dims, shards, -0.22, 0.18)
    return jnp.clip(strengthened(values, jax.random.fold_in(rng, 3), *heavy), -reach, reach).astype(kind)


def setup_inputs(seed: int = 0) -> dict:
    splits = jax.random.split(jax.random.key(seed), 7)
    return {
        "img_feat": gaussian_with(splits[0], (PAIRS, D), 1.0, 6.0, ((0, 32),), (0, 1, 32, 2.75)),
        "txt_feat": gaussian_with(splits[1], (PAIRS, D), 1.0, 6.0, ((0, 32),), (0, 1, 32, 2.75)),
        "img_weight": scatter_about(splits[2], (D, D), D ** -0.5, 0.1875),
        "txt_weight": scatter_about(splits[3], (D, D), D ** -0.5, 0.1875),
        "logit_scale": jnp.clip(jnp.exp(jax.random.uniform(splits[4], (1,), jnp.float32, math.log(5.0), math.log(20.0))), 5.0, 20.0),
        "logit_bias": jnp.clip(jax.random.uniform(splits[5], (1,), jnp.float32, -2.0, 0.0), -2.0, 0.0),
    }


def embed(feat, weight):
    proj = jnp.dot(feat, weight, preferred_element_type=jnp.float32)
    norm = jnp.sqrt(lax.optimization_barrier(jnp.sum(proj * proj, axis=1, keepdims=True)) + 1e-06)
    unit = proj / norm
    return (unit, unit.astype(jnp.bfloat16), norm)

def backward_unit(unit, direction, norm):
    along = lax.optimization_barrier(jnp.sum(unit * direction, axis=1, keepdims=True))
    return ((direction - unit * along) / norm).astype(jnp.bfloat16)

def reference(img_feat, txt_feat, img_weight, txt_weight, logit_scale, logit_bias):
    scale = logit_scale[0]
    bias = logit_bias[0]
    img_unit, img_emb, img_norm = embed(img_feat, img_weight)
    txt_unit, txt_emb, txt_norm = embed(txt_feat, txt_weight)
    count = img_emb.shape[0]
    eye = jnp.eye(count, dtype=jnp.float32)
    logits = scale * jnp.dot(img_emb, txt_emb.T, preferred_element_type=jnp.float32) + bias
    coef = (scale * (jax.nn.sigmoid(logits) - eye)).astype(jnp.bfloat16)
    img_dir = jnp.dot(coef, txt_emb, preferred_element_type=jnp.float32)
    txt_dir = jnp.dot(coef.T, img_emb, preferred_element_type=jnp.float32)
    img_back = backward_unit(img_unit, img_dir, img_norm)
    txt_back = backward_unit(txt_unit, txt_dir, txt_norm)
    grad_img_feat = jnp.dot(img_back, img_weight.T, preferred_element_type=jnp.float32).astype(jnp.bfloat16)
    grad_txt_feat = jnp.dot(txt_back, txt_weight.T, preferred_element_type=jnp.float32).astype(jnp.bfloat16)
    grad_img_weight = jnp.dot(img_feat.T, img_back, preferred_element_type=jnp.float32)
    grad_txt_weight = jnp.dot(txt_feat.T, txt_back, preferred_element_type=jnp.float32)
    return (grad_img_feat, grad_txt_feat, grad_img_weight, grad_txt_weight)
```

```python
import jax
import jax.numpy as jnp
from jax import lax
from jax.experimental import pallas as pl
from jax.experimental.pallas import tpu as pltpu
from jax.sharding import PartitionSpec as P

MESH = pl.DeviceIdType.MESH
F32 = jnp.float32
BF16 = jnp.bfloat16
D = 1152
BLOCK = 256
ROWS = 128
HALF = 64
OWN, RIGHT, LEFT, OPP = 0, 1, 2, 3
PART = 144
PIECE = 36
CUT = 80
COLS_A = 640
COLS_B = D - COLS_A


def nt(a, b):
    return lax.dot_general(a, b, (((1,), (1,)), ((), ())), preferred_element_type=F32)


def nn(a, b):
    return jnp.dot(a, b, preferred_element_type=F32)


def wrap(v):
    return lax.rem(v + 4, 4)


class Copies:
    def __init__(self, send, recv):
        self.send, self.recv, self.count = send, recv, 0

    def new(self, src, dst, device):
        k = self.count
        self.count += 1
        return pltpu.make_async_remote_copy(
            src_ref=src, dst_ref=dst, send_sem=self.send.at[k], recv_sem=self.recv.at[k],
            device_id=device, device_id_type=MESH,
        )


class RingSum:
    def __init__(self, copies, right, left, out, part, from_left, from_right, total, cut):
        self.out, self.part, self.total = out, part, total
        self.from_left, self.from_right, self.cut = from_left, from_right, cut
        rows = part.shape[1]
        lo, hi = pl.ds(0, cut), pl.ds(cut, rows - cut)
        self.lo, self.hi = lo, hi
        new = copies.new
        self.opp_r = new(out.at[2, lo], from_left, right)
        self.opp_l = new(out.at[2, hi], from_right, left)
        self.right_hi = new(out.at[0, hi], total.at[0, hi], right)
        self.left_lo = new(out.at[1, lo], total.at[1, lo], left)
        self.right_lo = new(out.at[0, lo], total.at[0, lo], right)
        self.left_hi = new(out.at[1, hi], total.at[1, hi], left)

    def send_opposite(self):
        self.opp_r.start()
        self.opp_l.start()

    def send_direct(self):
        self.out[0, self.hi, :] = self.part[0, self.hi, :].astype(BF16)
        self.right_hi.start()
        self.out[1, self.lo, :] = self.part[1, self.lo, :].astype(BF16)
        self.left_lo.start()

    def send_summed(self):
        self.opp_r.wait_recv()
        self.out[0, self.lo, :] = (
            self.part[0, self.lo, :] + self.from_left[...].astype(F32)
        ).astype(BF16)
        self.right_lo.start()
        self.opp_l.wait_recv()
        self.out[1, self.hi, :] = (
            self.part[1, self.hi, :] + self.from_right[...].astype(F32)
        ).astype(BF16)
        self.left_hi.start()

    def wait_total(self):
        self.left_lo.wait_recv()
        self.right_hi.wait_recv()
        self.right_lo.wait_recv()
        self.left_hi.wait_recv()

    def wait_sent(self):
        for c in (self.opp_r, self.opp_l, self.right_hi, self.left_lo, self.right_lo, self.left_hi):
            c.wait_send()


def kernel(
    img_feat, txt_feat, img_weight, txt_weight, logit_scale, logit_bias,
    out_img, out_txt, out_wi, out_wt,
    w, x_in, proj, unit, norm, img, txt, coef, coef_t,
    i_own, i_part, i_out, i_fl, i_fr, i_tot,
    t_own, t_part, t_out, t_fl, t_fr, t_tot, t_sib, t_sib_in,
    y_out, y_in, back, perm_a, perm_b, feat_grad, feat_far, feat_in,
    a_own, a_part, a_out, a_fl, a_fr, a_tot,
    b_own, b_part, b_out, b_fl, b_fr, b_tot,
    a2_out, a2_in, b2_out, b2_in, fin, y3_out, y3_in,
    load_sem, send_sem, recv_sem,
):
    blk = lax.axis_index("blk")
    rep = lax.axis_index("rep")
    z = blk // 8
    x = lax.rem(blk // 2, 4)
    y_hi = lax.rem(blk, 2)
    y_lo = rep // 2
    y = 2 * y_hi + y_lo
    core = lax.rem(rep, 2)

    def at(x_, y_, z_, core_):
        return {"blk": (z_ * 4 + x_) * 2 + y_ // 2, "rep": lax.rem(y_, 2) * 2 + core_}

    x_r, x_l, x_o = (at(wrap(x + d), y, z, core) for d in (1, -1, 2))
    z_r, z_l, z_o = (at(x, y, wrap(z + d), core) for d in (1, -1, 2))
    y_r, y_l, y_o = (at(x, wrap(y + d), z, core) for d in (1, -1, 2))
    sib = at(x, y, z, 1 - core)
    mate = {"blk": blk, "rep": lax.rem(rep + 2, 4)}

    barrier = pltpu.get_barrier_semaphore()
    for device in (x_r, x_l, x_o, z_r, z_l, z_o, y_r, y_l, y_o, sib):
        pl.semaphore_signal(barrier, inc=1, device_id=device, device_id_type=MESH)

    copies = Copies(send_sem, recv_sem)
    is_img = y_lo == 0
    is_txt = y_lo == 1

    load_xi = pltpu.make_async_copy(img_feat, x_in.at[0], load_sem.at[0])
    load_xt = pltpu.make_async_copy(txt_feat, x_in.at[1], load_sem.at[1])
    load_wi = pltpu.make_async_copy(img_weight, w.at[0], load_sem.at[2])
    load_wt = pltpu.make_async_copy(txt_weight, w.at[1], load_sem.at[3])

    @pl.when(is_txt)
    def _():
        load_xt.start()
        load_wt.start()

    load_xi.start()
    load_wi.start()

    own_lo = pl.ds(pl.multiple_of(core * HALF, HALF), HALF)
    own_hi = pl.ds(pl.multiple_of(ROWS + core * HALF, HALF), HALF)

    def project(tower):
        rows = jnp.concatenate([x_in[tower, own_lo, :], x_in[tower, own_hi, :]], axis=0)
        proj[...] = nn(rows, w[tower])
        p = proj[...]
        n = jnp.sqrt(jnp.sum(p * p, axis=1, keepdims=True) + 1e-06)
        return n, p / n

    def txt_rows(slot, c, start=0, size=ROWS):
        return txt.at[pl.ds(pl.multiple_of(slot * BLOCK + c * ROWS + start, HALF), size)]

    def img_rows(slot, start=0, size=ROWS):
        return img.at[pl.ds(slot * ROWS + start, size)]

    new = copies.new
    give_txt = [new(txt_rows(OWN, core, h, HALF), txt_rows(OWN, core, h, HALF), y_r) for h in (0, HALF)]

    def ring_gather(rows_of, right, left):
        lo, hi = (0, HALF), (HALF, HALF)
        return (
            new(rows_of(OWN, *lo), rows_of(LEFT, *lo), right),
            new(rows_of(OWN, *hi), rows_of(LEFT, *hi), right),
            new(rows_of(OWN, *hi), rows_of(RIGHT, *hi), left),
            new(rows_of(OWN, *lo), rows_of(RIGHT, *lo), left),
            new(rows_of(LEFT, *lo), rows_of(OPP, *lo), right),
            new(rows_of(RIGHT, *hi), rows_of(OPP, *hi), left),
        )

    gi = ring_gather(img_rows, x_r, x_l)
    gt = ring_gather(lambda s, a, n: txt_rows(s, core, a, n), z_r, z_l)
    share = [new(txt_rows(s, core), txt_rows(s, core), sib) for s in range(4)]

    @pl.when(is_txt)
    def _():
        load_xt.wait()
        load_wt.wait()
        n, u = project(1)
        unit[...] = u
        norm[...] = jnp.broadcast_to(n, norm.shape)
        txt_rows(OWN, core)[...] = u.astype(BF16)

    pl.semaphore_wait(barrier, 10)

    @pl.when(is_txt)
    def _():
        give_txt[0].start()
        give_txt[1].start()
        for c in gt[:4]:
            c.start()
        share[OWN].start()

    load_xi.wait()
    load_wi.wait()
    n, u = project(0)
    img_rows(OWN)[...] = u.astype(BF16)
    for c in gi[:4]:
        c.start()

    @pl.when(is_img)
    def _():
        unit[...] = u
        norm[...] = jnp.broadcast_to(n, norm.shape)
        give_txt[0].wait_recv()
        gt[0].start()
        gt[3].start()
        give_txt[1].wait_recv()
        gt[1].start()
        gt[2].start()
        share[OWN].start()

    def permuted(out, x_first):
        def step(q, _):
            r = lax.broadcasted_iota(jnp.int32, (PART, 1), 0)
            zero = r * 0
            inner = zero
            for j in range(1, 4):
                inner = inner + jnp.where(r >= PIECE * j, 1, 0)
            k = r - PIECE * inner
            yy = zero
            for j in range(1, 4):
                yy = yy + jnp.where(k >= 9 * j, 1, 0)
            i = k - 9 * yy

            def offset(s):
                return s + jnp.where(s == 2, 1, 0) - jnp.where(s == 3, 1, 0)

            outer = zero + q
            x_s, z_s = (outer, inner) if x_first else (inner, outer)
            xx = jnp.bitwise_and(x + offset(x_s), 3)
            zz = jnp.bitwise_and(z + offset(z_s), 3)
            source = 72 * (4 * zz + xx) + 18 * yy + 9 * core + i
            column = lax.broadcasted_iota(jnp.int32, (PART, D), 1)
            chosen = jnp.where(column == source, 1.0, 0.0).astype(BF16)
            at_rows = pl.ds(pl.multiple_of(q * PART, 16), PART)
            out[at_rows, :] = nt(chosen, x_in[y_lo]).astype(BF16)
            return 0

        lax.fori_loop(0, 4, step, 0)

    gi[0].wait_recv()
    gi[4].start()
    gi[2].wait_recv()
    gi[5].start()
    gt[0].wait_recv()
    gt[4].start()
    gt[2].wait_recv()
    gt[5].start()
    permuted(perm_a, True)
    permuted(perm_b, False)
    gt[1].wait_recv()
    share[LEFT].start()
    gt[3].wait_recv()
    share[RIGHT].start()
    gi[1].wait_recv()
    gi[3].wait_recv()

    scale = logit_scale[0]
    bias = logit_bias[0]

    def coefs(first, count, s):
        rows, cols = pl.ds(first * ROWS, count * ROWS), pl.ds(pl.multiple_of(s * BLOCK, BLOCK), BLOCK)
        logits = scale * nt(img[rows, :], txt[cols, :]) + bias
        value = jax.nn.sigmoid(logits)
        r = lax.broadcasted_iota(jnp.int32, value.shape, 0) + first * ROWS
        c = lax.broadcasted_iota(jnp.int32, value.shape, 1)
        on = jnp.where(jnp.logical_and(is_txt, s == OWN), 0, 4 * BLOCK)
        positive = jnp.where(r + core * ROWS == c + on, 1.0, 0.0)
        positive = jnp.where(r < ROWS, positive, 0.0)
        value = (scale * (value - positive)).astype(BF16)
        coef[rows, cols] = value
        coef_t[cols, rows] = value.T

    share[OWN].wait_recv()
    share[LEFT].wait_recv()
    share[RIGHT].wait_recv()

    def first_coefs(s, _):
        coefs(0, 3, s)
        return 0

    lax.fori_loop(0, 3, first_coefs, 0)

    gt[4].wait_recv()
    gt[5].wait_recv()
    share[OPP].start()
    gi[4].wait_recv()
    gi[5].wait_recv()

    def more_coefs(s, _):
        coefs(3, 1, s)
        return 0

    lax.fori_loop(0, 3, more_coefs, 0)
    share[OPP].wait_recv()
    coefs(0, 4, OPP)

    rx = RingSum(copies, x_r, x_l, i_out, i_part, i_fl, i_fr, i_tot, HALF)
    rz = RingSum(copies, z_r, z_l, t_out, t_part, t_fl, t_fr, t_tot, HALF)
    to_sib = [new(t_sib.at[s], t_sib_in.at[s], sib) for s in range(4)]

    my_half = pl.ds(pl.multiple_of(core * ROWS, ROWS), ROWS)
    its_half = pl.ds(pl.multiple_of((1 - core) * ROWS, ROWS), ROWS)

    def txt_sums(s):
        proj2 = nn(coef_t[s * BLOCK:(s + 1) * BLOCK, :], img[...])
        t_own[s] = proj2
        t_sib[s] = t_own[s, its_half, :].astype(BF16)
        to_sib[s].start()

    def txt_sum_of(s):
        to_sib[s].wait_recv()
        return t_own[s, my_half, :] + t_sib_in[s].astype(F32)

    txt_sums(OPP)
    i_out[2] = nn(coef[OPP * ROWS:(OPP + 1) * ROWS, :], txt[...]).astype(BF16)
    rx.send_opposite()
    txt_sums(RIGHT)
    txt_sums(LEFT)
    t_out[2] = txt_sum_of(OPP).astype(BF16)
    rz.send_opposite()
    both = nn(coef[ROWS:3 * ROWS, :], txt[...])
    i_part[0] = both[:ROWS]
    i_part[1] = both[ROWS:]
    rx.send_direct()
    t_part[0] = txt_sum_of(RIGHT)
    t_part[1] = txt_sum_of(LEFT)
    rz.send_direct()
    txt_sums(OWN)
    rx.send_summed()
    rz.send_summed()
    i_own[...] = nn(coef[:ROWS, :], txt[...])
    t_part[2] = txt_sum_of(OWN)

    hop = new(y_out, y_in, y_l)

    def whole(ring, own):
        ring.wait_total()
        return own + ring.total[0].astype(F32) + ring.total[1].astype(F32)

    @pl.when(is_img)
    def _():
        y_out[...] = whole(rz, t_part[2]).astype(BF16)
        hop.start()
        proj[...] = whole(rx, i_own[...])

    @pl.when(is_txt)
    def _():
        y_out[...] = whole(rx, i_own[...]).astype(BF16)
        hop.start()
        proj[...] = whole(rz, t_part[2])

    hop.wait_recv()
    direction = proj[...] + y_in[...].astype(F32)
    u_own = unit[...]
    along = jnp.sum(u_own * direction, axis=1, keepdims=True)
    mine = ((direction - u_own * along) / norm[:, :1]).astype(BF16)
    back[own_lo, :] = mine[:HALF]
    back[own_hi, :] = mine[HALF:]
    give_back = [new(back.at[own_lo], back.at[own_lo], sib), new(back.at[own_hi], back.at[own_hi], sib)]
    give_back[0].start()
    give_back[1].start()
    give_back[0].wait_recv()
    give_back[1].wait_recv()

    ra = RingSum(copies, x_r, x_l, a_out, a_part, a_fl, a_fr, a_tot, CUT)
    rb = RingSum(copies, z_r, z_l, b_out, b_part, b_fl, b_fr, b_tot, CUT)

    def part_a(s):
        return nn(perm_a[s * PART:(s + 1) * PART, :], back[:, :COLS_A])

    def part_b(s):
        return nn(perm_b[s * PART:(s + 1) * PART, :], back[:, COLS_A:])

    a_out[2] = part_a(OPP).astype(BF16)
    ra.send_opposite()
    b_out[2] = part_b(OPP).astype(BF16)
    rb.send_opposite()
    a_part[0] = part_a(RIGHT)
    a_part[1] = part_a(LEFT)
    ra.send_direct()
    b_part[0] = part_b(RIGHT)
    b_part[1] = part_b(LEFT)
    rb.send_direct()
    a_own[:PART, :] = part_a(OWN)
    b_own[:PART, :] = part_b(OWN)
    a_own[PART:, :] = jnp.zeros((16, COLS_A), F32)
    b_own[PART:, :] = jnp.zeros((16, COLS_B), F32)
    ra.send_summed()
    rb.send_summed()

    grad = nt(jnp.concatenate([back[own_lo, :], back[own_hi, :]], axis=0), w[y_lo]).astype(BF16)
    feat_grad[0] = grad[:HALF]
    feat_grad[1] = grad[HALF:]
    give_grad = new(feat_grad.at[1 - y_lo], feat_in, mate)
    give_grad.start()

    ra.wait_total()
    a_own[:PART, :] = a_own[:PART, :] + a_tot[0].astype(F32) + a_tot[1].astype(F32)

    def second(own, out, inbox, right, left, opposite):
        sends = []
        for s, there, device in ((OPP, OPP, opposite), (RIGHT, LEFT, right), (LEFT, RIGHT, left)):
            out[s] = own[s * PIECE:s * PIECE + 48, :].astype(BF16)
            c = new(out.at[s], inbox.at[there], device)
            c.start()
            sends.append(c)
        return sends

    sa = second(a_own, a2_out, a2_in, z_r, z_l, z_o)
    rb.wait_total()
    b_own[:PART, :] = b_own[:PART, :] + b_tot[0].astype(F32) + b_tot[1].astype(F32)
    sb = second(b_own, b2_out, b2_in, x_r, x_l, x_o)

    for c in sa:
        c.wait_recv()
    fin[:, :COLS_A] = (
        a_own[:48, :] + a2_in[1].astype(F32) + a2_in[2].astype(F32) + a2_in[3].astype(F32)
    )
    for c in sb:
        c.wait_recv()
    fin[:, COLS_A:] = (
        b_own[:48, :] + b2_in[1].astype(F32) + b2_in[2].astype(F32) + b2_in[3].astype(F32)
    )

    for j in range(4):
        y3_out[j] = fin[9 * j:9 * j + 16, :].astype(BF16)
    s3 = []
    for d, device in ((2, y_o), (1, y_r), (3, y_l)):
        c = new(y3_out.at[wrap(y + d)], y3_in.at[y], device)
        c.start()
        s3.append(c)
    y3_in[y] = y3_out[y]

    give_grad.wait_recv()

    @pl.when(is_img)
    def _():
        out_img[...] = feat_grad[0]
        out_txt[...] = feat_in[...]

    @pl.when(is_txt)
    def _():
        out_img[...] = feat_in[...]
        out_txt[...] = feat_grad[1]

    for c in s3:
        c.wait_recv()
    out_wi[...] = (y3_in[0].astype(F32) + y3_in[2].astype(F32))[:9]
    out_wt[...] = (y3_in[1].astype(F32) + y3_in[3].astype(F32))[:9]

    @pl.when(is_txt)
    def _():
        give_txt[0].wait_send()
        give_txt[1].wait_send()

    for c in (*gi, *gt, *share, *to_sib, hop, *give_back, give_grad, *sa, *sb, *s3):
        c.wait_send()
    for ring in (rx, rz, ra, rb):
        ring.wait_sent()


def ring_scratch(rows, cols, cut):
    return [
        pltpu.VMEM((3, rows, cols), BF16),
        pltpu.VMEM((cut, cols), BF16),
        pltpu.VMEM((rows - cut, cols), BF16),
        pltpu.VMEM((2, rows, cols), BF16),
    ]


N_COPIES = 80


def per_device(img_feat, txt_feat, img_weight, txt_weight, logit_scale, logit_bias):
    anywhere = pl.BlockSpec(memory_space=pl.ANY)
    scalar = pl.BlockSpec(memory_space=pltpu.SMEM)
    vmem = pl.BlockSpec(memory_space=pltpu.VMEM)
    V = pltpu.VMEM
    return pl.pallas_call(
        kernel,
        name="pair_gradients",
        out_shape=(
            jax.ShapeDtypeStruct((HALF, D), BF16),
            jax.ShapeDtypeStruct((HALF, D), BF16),
            jax.ShapeDtypeStruct((9, D), F32),
            jax.ShapeDtypeStruct((9, D), F32),
        ),
        in_specs=[anywhere] * 4 + [scalar] * 2,
        out_specs=(vmem,) * 4,
        scratch_shapes=[
            V((2, D, D), BF16),
            V((2, BLOCK, D), BF16),
            V((ROWS, D), F32),
            V((ROWS, D), F32),
            V((ROWS, 128), F32),
            V((4 * ROWS, D), BF16),
            V((4 * BLOCK, D), BF16),
            V((4 * ROWS, 4 * BLOCK), BF16),
            V((4 * BLOCK, 4 * ROWS), BF16),
            V((ROWS, D), F32),
            V((2, ROWS, D), F32),
            *ring_scratch(ROWS, D, HALF),
            V((4, BLOCK, D), F32),
            V((3, ROWS, D), F32),
            *ring_scratch(ROWS, D, HALF),
            V((4, ROWS, D), BF16),
            V((4, ROWS, D), BF16),
            V((ROWS, D), BF16),
            V((ROWS, D), BF16),
            V((BLOCK, D), BF16),
            V((4 * PART, BLOCK), BF16),
            V((4 * PART, BLOCK), BF16),
            V((2, HALF, D), BF16),
            V((2, HALF, D), BF16),
            V((HALF, D), BF16),
            V((PART + 16, COLS_A), F32),
            V((2, PART, COLS_A), F32),
            *ring_scratch(PART, COLS_A, CUT),
            V((PART + 16, COLS_B), F32),
            V((2, PART, COLS_B), F32),
            *ring_scratch(PART, COLS_B, CUT),
            V((4, 48, COLS_A), BF16),
            V((4, 48, COLS_A), BF16),
            V((4, 48, COLS_B), BF16),
            V((4, 48, COLS_B), BF16),
            V((48, D), F32),
            V((4, 16, D), BF16),
            V((4, 16, D), BF16),
            pltpu.SemaphoreType.DMA((4,)),
            pltpu.SemaphoreType.DMA((N_COPIES,)),
            pltpu.SemaphoreType.DMA((N_COPIES,)),
        ],
        compiler_params=pltpu.CompilerParams(
            collective_id=0, has_side_effects=True, vmem_limit_bytes=60 * 1024 * 1024
        ),
        cost_estimate=pl.CostEstimate(
            flops=6_000_000_000, bytes_accessed=8_000_000, transcendentals=600_000
        ),
    )(img_feat, txt_feat, img_weight, txt_weight, logit_scale, logit_bias)


def solution(mesh):
    placed = (P("blk", None), P("blk", None), P(), P(), P(), P())
    return jax.shard_map(
        per_device,
        mesh=mesh,
        in_specs=placed,
        out_specs=(P(("blk", "rep"), None),) * 4,
        check_vma=False,
    )
```

```python
import jax
import jax.numpy as jnp
from jax import lax
from jax.experimental import pallas as pl
from jax.experimental.pallas import tpu as pltpu
from jax.sharding import PartitionSpec as P

MESH = pl.DeviceIdType.MESH
F32 = jnp.float32
BF16 = jnp.bfloat16
D = 1152
BLOCK = 256
ROWS = 128
HALF = 64
OWN, RIGHT, LEFT, OPP = 0, 1, 2, 3
PART = 144
PIECE = 36
CUT = 80
COLS_A = 640
COLS_B = D - COLS_A
GATHER = 2
PASSES = 2


def nt(a, b):
    return lax.dot_general(a, b, (((1,), (1,)), ((), ())), preferred_element_type=F32)


def nn(a, b):
    return jnp.dot(a, b, preferred_element_type=F32)


def wrap(v):
    return lax.rem(v + 4, 4)


class Copies:
    def __init__(self, send, recv):
        self.send, self.recv, self.count = send, recv, 0

    def new(self, src, dst, device):
        k = self.count
        self.count += 1
        return pltpu.make_async_remote_copy(
            src_ref=src, dst_ref=dst, send_sem=self.send.at[k], recv_sem=self.recv.at[k],
            device_id=device, device_id_type=MESH,
        )


class RingSum:
    def __init__(self, copies, right, left, out, part, mid, total, start, rows, cut):
        self.out, self.part, self.mid, self.total = out, part, mid, total
        lo, hi = pl.ds(start, cut), pl.ds(start + cut, rows - cut)
        self.lo, self.hi, self.rows = lo, hi, pl.ds(start, rows)
        new = copies.new
        self.opp_r = new(out.at[2, lo], mid.at[lo], right)
        self.opp_l = new(out.at[2, hi], mid.at[hi], left)
        self.right_hi = new(out.at[0, hi], total.at[0, hi], right)
        self.left_lo = new(out.at[1, lo], total.at[1, lo], left)
        self.right_lo = new(out.at[0, lo], total.at[0, lo], right)
        self.left_hi = new(out.at[1, hi], total.at[1, hi], left)

    def send_opposite(self):
        self.opp_r.start()
        self.opp_l.start()

    def send_direct(self):
        self.out[0, self.hi, :] = self.part[0, self.hi, :].astype(BF16)
        self.right_hi.start()
        self.out[1, self.lo, :] = self.part[1, self.lo, :].astype(BF16)
        self.left_lo.start()

    def send_summed(self):
        self.opp_r.wait_recv()
        self.out[0, self.lo, :] = (
            self.part[0, self.lo, :] + self.mid[self.lo, :].astype(F32)
        ).astype(BF16)
        self.right_lo.start()
        self.opp_l.wait_recv()
        self.out[1, self.hi, :] = (
            self.part[1, self.hi, :] + self.mid[self.hi, :].astype(F32)
        ).astype(BF16)
        self.left_hi.start()

    def received(self):
        self.left_lo.wait_recv()
        self.right_hi.wait_recv()
        self.right_lo.wait_recv()
        self.left_hi.wait_recv()
        return self.total[0, self.rows, :].astype(F32) + self.total[1, self.rows, :].astype(F32)

    def wait_sent(self):
        for c in (self.opp_r, self.opp_l, self.right_hi, self.left_lo, self.right_lo, self.left_hi):
            c.wait_send()


def kernel(
    img_feat, txt_feat, img_weight, txt_weight, logit_scale, logit_bias,
    out_img, out_txt, out_wi, out_wt,
    w, x_in, proj, unit, norm, ours, other, coef_a, coef_b,
    a_own, a_part, a_out, a_mid, a_tot,
    b_own, b_part, b_out, b_mid, b_tot,
    y_out, y_in, back, perm_a, perm_b, feat_grad, feat_in,
    wa_own, wa_part, wa_out, wa_mid, wa_tot,
    wb_own, wb_part, wb_out, wb_mid, wb_tot,
    wa2_out, wa2_in, wb2_out, wb2_in, fin, y3_out, y3_in,
    load_sem, send_sem, recv_sem,
):
    blk = lax.axis_index("blk")
    rep = lax.axis_index("rep")
    z = blk // 8
    x = lax.rem(blk // 2, 4)
    y_hi = lax.rem(blk, 2)
    y_lo = rep // 2
    y = 2 * y_hi + y_lo
    core = lax.rem(rep, 2)

    def at(x_, y_, z_, core_):
        return {"blk": (z_ * 4 + x_) * 2 + y_ // 2, "rep": lax.rem(y_, 2) * 2 + core_}

    x_r, x_l, x_o = (at(wrap(x + d), y, z, core) for d in (1, -1, 2))
    z_r, z_l, z_o = (at(x, y, wrap(z + d), core) for d in (1, -1, 2))
    y_r, y_l, y_o = (at(x, wrap(y + d), z, core) for d in (1, -1, 2))
    sib = at(x, y, z, 1 - core)
    mate = {"blk": blk, "rep": lax.rem(rep + 2, 4)}
    a_r, a_l = (at(wrap(x + d * (1 - y_lo)), y, wrap(z + d * y_lo), core) for d in (1, -1))
    b_r, b_l = (at(wrap(x + d * y_lo), y, wrap(z + d * (1 - y_lo)), core) for d in (1, -1))

    barrier = pltpu.get_barrier_semaphore()
    for device in (x_r, x_l, x_o, z_r, z_l, z_o, y_r, y_l, y_o, sib):
        pl.semaphore_signal(barrier, inc=1, device_id=device, device_id_type=MESH)

    copies = Copies(send_sem, recv_sem)
    is_img = y_lo == 0
    is_txt = y_lo == 1

    load_img = [pltpu.make_async_copy(img_feat, x_in.at[0], load_sem.at[0]),
                pltpu.make_async_copy(img_weight, w.at[0], load_sem.at[1])]
    load_txt = [pltpu.make_async_copy(txt_feat, x_in.at[0], load_sem.at[0]),
                pltpu.make_async_copy(txt_weight, w.at[0], load_sem.at[1])]
    load_other = [pltpu.make_async_copy(img_feat, x_in.at[1], load_sem.at[2]),
                  pltpu.make_async_copy(img_weight, w.at[1], load_sem.at[3])]

    @pl.when(is_img)
    def _():
        for c in load_img:
            c.start()

    @pl.when(is_txt)
    def _():
        for c in (*load_txt, *load_other):
            c.start()

    own_lo = pl.ds(pl.multiple_of(core * HALF, HALF), HALF)
    own_hi = pl.ds(pl.multiple_of(ROWS + core * HALF, HALF), HALF)

    def project(k):
        rows = jnp.concatenate([x_in[k, own_lo, :], x_in[k, own_hi, :]], axis=0)
        proj[...] = nn(rows, w[k])
        p = proj[...]
        n = jnp.sqrt(jnp.sum(p * p, axis=1, keepdims=True) + 1e-06)
        return n, p / n

    def rows_at(ref, slot, c, begin=0, size=ROWS):
        return ref.at[pl.ds(pl.multiple_of(slot * BLOCK + c * ROWS + begin, 16), size)]

    new = copies.new
    chunk = ROWS // GATHER
    give = [
        new(rows_at(ours, OWN, core, q * chunk, chunk), rows_at(other, OWN, core, q * chunk, chunk), y_r)
        for q in range(GATHER)
    ]

    class RingGather:
        def __init__(self, ref, right, left):
            def of(slot, q):
                return rows_at(ref, slot, core, q * chunk, chunk)

            every = range(GATHER)
            self.to_right = [new(of(OWN, q), of(LEFT, q), right) for q in every]
            self.to_left = [new(of(OWN, q), of(RIGHT, q), left) for q in every]
            self.onward = [
                new(of(LEFT, q), of(OPP, q), right) if q < GATHER // 2
                else new(of(RIGHT, q), of(OPP, q), left)
                for q in every
            ]

        def send(self, q):
            first, second = self.to_right[q], self.to_left[q]
            if q >= GATHER // 2:
                first, second = second, first
            first.start()
            second.start()

        def forward(self, q):
            (self.to_right if q < GATHER // 2 else self.to_left)[q].wait_recv()
            self.onward[q].start()

        def wait_near(self):
            for q in range(GATHER):
                (self.to_left if q < GATHER // 2 else self.to_right)[q].wait_recv()

        def wait_far(self):
            for c in self.onward:
                c.wait_recv()

        def wait_sent(self):
            for c in (*self.to_right, *self.to_left, *self.onward):
                c.wait_send()

    ga = RingGather(ours, a_r, a_l)
    gb = RingGather(other, b_r, b_l)
    share_a = [new(rows_at(ours, s, core), rows_at(ours, s, core), sib) for s in range(4)]
    share_b = [new(rows_at(other, s, core), rows_at(other, s, core), sib) for s in range(4)]
    order = []
    for q in range(GATHER // 2):
        order += [q, GATHER - 1 - q]

    for c in load_img:
        c.wait()
    n, u = project(0)
    unit[...] = u
    norm[...] = jnp.broadcast_to(n, norm.shape)
    rows_at(ours, OWN, core)[...] = u.astype(BF16)

    pl.semaphore_wait(barrier, 10)

    @pl.when(is_txt)
    def _():
        for q in order:
            give[q].start()

    for q in order:
        ga.send(q)
    share_a[OWN].start()

    @pl.when(is_txt)
    def _():
        for c in load_other:
            c.wait()
        _, v = project(1)
        rows_at(other, OWN, core)[...] = v.astype(BF16)
        for q in order:
            gb.send(q)

    def pass_on(q):
        @pl.when(is_img)
        def _():
            give[q].wait_recv()
            gb.send(q)

    early, late = order[:GATHER // 2], order[GATHER // 2:]
    for q in early:
        ga.forward(q)
    for q in early:
        pass_on(q)
    for q in late:
        ga.forward(q)
    for q in late:
        pass_on(q)
    share_b[OWN].start()

    def permuted(out, x_first):
        def step(q, _):
            r = lax.broadcasted_iota(jnp.int32, (PART, 1), 0)
            zero = r * 0
            inner = zero
            for j in range(1, 4):
                inner = inner + jnp.where(r >= PIECE * j, 1, 0)
            k = r - PIECE * inner
            yy = zero
            for j in range(1, 4):
                yy = yy + jnp.where(k >= 9 * j, 1, 0)
            i = k - 9 * yy

            def offset(s):
                return s + jnp.where(s == 2, 1, 0) - jnp.where(s == 3, 1, 0)

            outer = zero + q
            x_s, z_s = (outer, inner) if x_first else (inner, outer)
            xx = jnp.bitwise_and(x + offset(x_s), 3)
            zz = jnp.bitwise_and(z + offset(z_s), 3)
            source = 72 * (4 * zz + xx) + 18 * yy + 9 * core + i
            column = lax.broadcasted_iota(jnp.int32, (PART, D), 1)
            chosen = jnp.where(column == source, 1.0, 0.0).astype(BF16)
            at_rows = pl.ds(pl.multiple_of(q * PART, 16), PART)
            out[at_rows, :] = nt(chosen, x_in[0]).astype(BF16)
            return 0

        lax.fori_loop(0, 4, step, 0)

    permuted(perm_a, True)
    for q in order:
        gb.forward(q)
    permuted(perm_b, False)
    ga.wait_near()
    share_a[LEFT].start()
    share_a[RIGHT].start()
    ga.wait_far()
    share_a[OPP].start()

    half = 0.5 * logit_scale[0]
    half_bias = 0.5 * logit_bias[0]

    def coefs(out, rows_of, cols_of, first, count, s, slots):
        rows = jnp.concatenate([rows_at(rows_of, k, core)[...] for k in range(first, first + count)], axis=0)
        cols = pl.ds(s * BLOCK, slots * BLOCK)
        value = half * jnp.tanh(half * nt(rows, cols_of[cols, :]) + half_bias) + half
        out[pl.ds(first * ROWS, count * ROWS), cols] = value.astype(BF16)

    def matching(out, rows_of, cols_of):
        value = half * jnp.tanh(half * nt(rows_at(rows_of, OWN, core)[...], rows_at(cols_of, OWN, core)[...]) + half_bias)
        r = lax.broadcasted_iota(jnp.int32, value.shape, 0)
        c = lax.broadcasted_iota(jnp.int32, value.shape, 1)
        value = jnp.where(r == c, value - half, value + half)
        out[:ROWS, pl.ds(pl.multiple_of(core * ROWS, ROWS), ROWS)] = value.astype(BF16)

    share_b[OWN].wait_recv()
    coefs(coef_a, ours, other, 0, 4, OWN, 1)
    for c in share_a:
        c.wait_recv()
    coefs(coef_b, other, ours, OWN, 1, 0, 4)

    @pl.when(is_txt)
    def _():
        matching(coef_a, ours, other)
        matching(coef_b, other, ours)

    gb.wait_near()
    share_b[LEFT].start()
    share_b[RIGHT].start()
    coefs(coef_b, other, ours, RIGHT, 2, 0, 4)
    share_b[LEFT].wait_recv()
    share_b[RIGHT].wait_recv()
    coefs(coef_a, ours, other, 0, 4, RIGHT, 2)
    gb.wait_far()
    share_b[OPP].start()

    size = ROWS // PASSES
    blocks = [pl.ds(h * size, size) for h in range(PASSES)]
    ra = [RingSum(copies, a_r, a_l, a_out, a_part, a_mid, a_tot, h * size, size, size // 2) for h in range(PASSES)]
    rb = [RingSum(copies, b_r, b_l, b_out, b_part, b_mid, b_tot, h * size, size, size // 2) for h in range(PASSES)]

    coefs(coef_b, other, ours, OPP, 1, 0, 4)
    b_out[2] = nn(coef_b[OPP * ROWS:, :], ours[...]).astype(BF16)
    for ring in rb:
        ring.send_opposite()
    share_b[OPP].wait_recv()
    coefs(coef_a, ours, other, 0, 4, OPP, 1)
    a_out[2] = nn(coef_a[OPP * ROWS:, :], other[...]).astype(BF16)
    for ring in ra:
        ring.send_opposite()
    both = nn(coef_b[ROWS:3 * ROWS, :], ours[...])
    b_part[0] = both[:ROWS]
    b_part[1] = both[ROWS:]
    rb[0].send_direct()
    both = nn(coef_a[ROWS:3 * ROWS, :], other[...])
    a_part[0] = both[:ROWS]
    a_part[1] = both[ROWS:]
    ra[0].send_direct()
    rb[0].send_summed()
    ra[0].send_summed()
    for h in range(1, PASSES):
        rb[h].send_direct()
        ra[h].send_direct()
    b_own[...] = nn(coef_b[:ROWS, :], ours[...])
    a_own[...] = nn(coef_a[:ROWS, :], other[...])
    for h in range(1, PASSES):
        rb[h].send_summed()
        ra[h].send_summed()

    hop = [new(y_out.at[b], y_in.at[b], y_l) for b in blocks]
    give_back = []
    for h, b in enumerate(blocks):
        y_out[b, :] = (b_own[b, :] + rb[h].received()).astype(BF16)
        hop[h].start()
        proj[b, :] = a_own[b, :] + ra[h].received()

    for h, b in enumerate(blocks):
        hop[h].wait_recv()
        direction = proj[b, :] + y_in[b, :].astype(F32)
        u_own = unit[b, :]
        along = jnp.sum(u_own * direction, axis=1, keepdims=True)
        mine = ((direction - u_own * along) / norm[b, :1]).astype(BF16)
        begin = h * size
        where = pl.ds(pl.multiple_of((begin // HALF) * ROWS + core * HALF + begin % HALF, 32), size)
        back[where, :] = mine
        c = new(back.at[where], back.at[where], sib)
        c.start()
        give_back.append(c)
    for c in give_back:
        c.wait_recv()

    wa = RingSum(copies, x_r, x_l, wa_out, wa_part, wa_mid, wa_tot, 0, PART, CUT)
    wb = RingSum(copies, z_r, z_l, wb_out, wb_part, wb_mid, wb_tot, 0, PART, CUT)

    def part_a(s):
        return nn(perm_a[s * PART:(s + 1) * PART, :], back[:, :COLS_A])

    def part_b(s):
        return nn(perm_b[s * PART:(s + 1) * PART, :], back[:, COLS_A:])

    wa_out[2] = part_a(OPP).astype(BF16)
    wa.send_opposite()
    wb_out[2] = part_b(OPP).astype(BF16)
    wb.send_opposite()
    wa_part[0] = part_a(RIGHT)
    wa_part[1] = part_a(LEFT)
    wa.send_direct()
    wb_part[0] = part_b(RIGHT)
    wb_part[1] = part_b(LEFT)
    wb.send_direct()
    wa_own[:PART, :] = part_a(OWN)
    wb_own[:PART, :] = part_b(OWN)
    wa_own[PART:, :] = jnp.zeros((16, COLS_A), F32)
    wb_own[PART:, :] = jnp.zeros((16, COLS_B), F32)
    wa.send_summed()
    wb.send_summed()

    grad = nt(jnp.concatenate([back[own_lo, :], back[own_hi, :]], axis=0), w[0]).astype(BF16)
    feat_grad[0] = grad[:HALF]
    feat_grad[1] = grad[HALF:]
    give_grad = new(feat_grad.at[1 - y_lo], feat_in, mate)
    give_grad.start()

    wa_own[:PART, :] = wa_own[:PART, :] + wa.received()

    def second(own, out, inbox, right, left, opposite):
        sends = []
        for s, there, device in ((OPP, OPP, opposite), (RIGHT, LEFT, right), (LEFT, RIGHT, left)):
            out[s] = own[s * PIECE:s * PIECE + 48, :].astype(BF16)
            c = new(out.at[s], inbox.at[there], device)
            c.start()
            sends.append(c)
        return sends

    sa = second(wa_own, wa2_out, wa2_in, z_r, z_l, z_o)
    wb_own[:PART, :] = wb_own[:PART, :] + wb.received()
    sb = second(wb_own, wb2_out, wb2_in, x_r, x_l, x_o)

    for c in sa:
        c.wait_recv()
    fin[:, :COLS_A] = (
        wa_own[:48, :] + wa2_in[1].astype(F32) + wa2_in[2].astype(F32) + wa2_in[3].astype(F32)
    )
    for c in sb:
        c.wait_recv()
    fin[:, COLS_A:] = (
        wb_own[:48, :] + wb2_in[1].astype(F32) + wb2_in[2].astype(F32) + wb2_in[3].astype(F32)
    )

    for j in range(4):
        y3_out[j] = fin[9 * j:9 * j + 16, :].astype(BF16)
    s3 = []
    for d, device in ((2, y_o), (1, y_r), (3, y_l)):
        c = new(y3_out.at[wrap(y + d)], y3_in.at[y], device)
        c.start()
        s3.append(c)
    y3_in[y] = y3_out[y]

    give_grad.wait_recv()

    @pl.when(is_img)
    def _():
        out_img[...] = feat_grad[0]
        out_txt[...] = feat_in[...]

    @pl.when(is_txt)
    def _():
        out_img[...] = feat_in[...]
        out_txt[...] = feat_grad[1]

    for c in s3:
        c.wait_recv()
    out_wi[...] = (y3_in[0].astype(F32) + y3_in[2].astype(F32))[:9]
    out_wt[...] = (y3_in[1].astype(F32) + y3_in[3].astype(F32))[:9]

    @pl.when(is_txt)
    def _():
        for c in give:
            c.wait_send()

    for c in (*share_a, *share_b, *hop, *give_back, give_grad, *sa, *sb, *s3):
        c.wait_send()
    for ring in (ga, gb, *ra, *rb, wa, wb):
        ring.wait_sent()


def hand_out(a, b, c, d, out_a, out_b, out_c, out_d):
    for src, dst in ((a, out_a), (b, out_b), (c, out_c), (d, out_d)):
        dst[...] = src[...]


def ring_scratch(rows, cols):
    return [
        pltpu.VMEM((3, rows, cols), BF16),
        pltpu.VMEM((rows, cols), BF16),
        pltpu.VMEM((2, rows, cols), BF16),
    ]


N_COPIES = 112


def per_device(img_feat, txt_feat, img_weight, txt_weight, logit_scale, logit_bias):
    anywhere = pl.BlockSpec(memory_space=pl.ANY)
    vmem = pl.BlockSpec(memory_space=pltpu.VMEM)
    V = pltpu.VMEM
    outs = pl.pallas_call(
        kernel,
        name="pair_gradients",
        out_shape=(
            pltpu.VMEM((HALF, D), BF16),
            pltpu.VMEM((HALF, D), BF16),
            pltpu.VMEM((9, D), F32),
            pltpu.VMEM((9, D), F32),
        ),
        in_specs=[anywhere] * 4 + [pl.BlockSpec(memory_space=pltpu.SMEM)] * 2,
        out_specs=(vmem,) * 4,
        scratch_shapes=[
            V((2, D, D), BF16),
            V((2, BLOCK, D), BF16),
            V((ROWS, D), F32),
            V((ROWS, D), F32),
            V((ROWS, 128), F32),
            V((4 * BLOCK, D), BF16),
            V((4 * BLOCK, D), BF16),
            V((4 * ROWS, 4 * BLOCK), BF16),
            V((4 * ROWS, 4 * BLOCK), BF16),
            V((ROWS, D), F32),
            V((2, ROWS, D), F32),
            *ring_scratch(ROWS, D),
            V((ROWS, D), F32),
            V((2, ROWS, D), F32),
            *ring_scratch(ROWS, D),
            V((ROWS, D), BF16),
            V((ROWS, D), BF16),
            V((BLOCK, D), BF16),
            V((4 * PART, BLOCK), BF16),
            V((4 * PART, BLOCK), BF16),
            V((2, HALF, D), BF16),
            V((HALF, D), BF16),
            V((PART + 16, COLS_A), F32),
            V((2, PART, COLS_A), F32),
            *ring_scratch(PART, COLS_A),
            V((PART + 16, COLS_B), F32),
            V((2, PART, COLS_B), F32),
            *ring_scratch(PART, COLS_B),
            V((4, 48, COLS_A), BF16),
            V((4, 48, COLS_A), BF16),
            V((4, 48, COLS_B), BF16),
            V((4, 48, COLS_B), BF16),
            V((48, D), F32),
            V((4, 16, D), BF16),
            V((4, 16, D), BF16),
            pltpu.SemaphoreType.DMA((4,)),
            pltpu.SemaphoreType.DMA((N_COPIES,)),
            pltpu.SemaphoreType.DMA((N_COPIES,)),
        ],
        compiler_params=pltpu.CompilerParams(
            collective_id=0, has_side_effects=True, vmem_limit_bytes=60 * 1024 * 1024
        ),
        cost_estimate=pl.CostEstimate(
            flops=6_000_000_000, bytes_accessed=8_000_000, transcendentals=600_000
        ),
    )(
        img_feat, txt_feat, img_weight, txt_weight,
        logit_scale, logit_bias,
    )
    return pl.pallas_call(
        hand_out,
        name="hand_out",
        out_shape=tuple(jax.ShapeDtypeStruct(o.shape, o.dtype) for o in outs),
        in_specs=[vmem] * 4,
        out_specs=(vmem,) * 4,
        compiler_params=pltpu.CompilerParams(vmem_limit_bytes=4 * 1024 * 1024),
    )(*outs)


def solution(mesh):
    placed = (P("blk", None), P("blk", None), P(), P(), P(), P())
    return jax.shard_map(
        per_device,
        mesh=mesh,
        in_specs=placed,
        out_specs=(P(("blk", "rep"), None),) * 4,
        check_vma=False,
    )
```

```python
import jax
import jax.numpy as jnp
from jax import lax
from jax.experimental import pallas as pl
from jax.experimental.pallas import tpu as pltpu
from jax.sharding import PartitionSpec as P

MESH = pl.DeviceIdType.MESH
F32 = jnp.float32
BF16 = jnp.bfloat16
D = 1152
BLOCK = 256
ROWS = 128
HALF = 64
OWN, RIGHT, LEFT, OPP = 0, 1, 2, 3
PART = 144
PIECE = 36
CUT = 80
COLS_A = 640
COLS_B = D - COLS_A
DEEP = 512
GIVE = 2
GATHER = 2
PASSES = 2


def nt(a, b):
    return lax.dot_general(a, b, (((1,), (1,)), ((), ())), preferred_element_type=F32)


def nn(a, b):
    return jnp.dot(a, b, preferred_element_type=F32)


def wrap(v):
    return lax.rem(v + 4, 4)


class Copies:
    def __init__(self, send, recv):
        self.send, self.recv, self.count = send, recv, 0

    def new(self, src, dst, device):
        k = self.count
        self.count += 1
        return pltpu.make_async_remote_copy(
            src_ref=src, dst_ref=dst, send_sem=self.send.at[k], recv_sem=self.recv.at[k],
            device_id=device, device_id_type=MESH,
        )


class RingSum:
    def __init__(self, copies, right, left, out, part, mid, total, start, rows, cut):
        self.out, self.part, self.mid, self.total = out, part, mid, total
        lo, hi = pl.ds(start, cut), pl.ds(start + cut, rows - cut)
        self.lo, self.hi, self.rows = lo, hi, pl.ds(start, rows)
        new = copies.new
        self.opp_r = new(out.at[2, lo], mid.at[lo], right)
        self.opp_l = new(out.at[2, hi], mid.at[hi], left)
        self.right_hi = new(out.at[0, hi], total.at[0, hi], right)
        self.left_lo = new(out.at[1, lo], total.at[1, lo], left)
        self.right_lo = new(out.at[0, lo], total.at[0, lo], right)
        self.left_hi = new(out.at[1, hi], total.at[1, hi], left)

    def send_opposite(self):
        self.opp_r.start()
        self.opp_l.start()

    def send_direct(self):
        self.out[0, self.hi, :] = self.part[0, self.hi, :].astype(BF16)
        self.right_hi.start()
        self.out[1, self.lo, :] = self.part[1, self.lo, :].astype(BF16)
        self.left_lo.start()

    def send_summed(self):
        self.opp_r.wait_recv()
        self.out[0, self.lo, :] = (
            self.part[0, self.lo, :] + self.mid[self.lo, :].astype(F32)
        ).astype(BF16)
        self.right_lo.start()
        self.opp_l.wait_recv()
        self.out[1, self.hi, :] = (
            self.part[1, self.hi, :] + self.mid[self.hi, :].astype(F32)
        ).astype(BF16)
        self.left_hi.start()

    def received(self):
        self.left_lo.wait_recv()
        self.right_hi.wait_recv()
        self.right_lo.wait_recv()
        self.left_hi.wait_recv()
        return self.total[0, self.rows, :].astype(F32) + self.total[1, self.rows, :].astype(F32)

    def wait_sent(self):
        for c in (self.opp_r, self.opp_l, self.right_hi, self.left_lo, self.right_lo, self.left_hi):
            c.wait_send()


def kernel(
    img_feat, txt_feat, img_weight, txt_weight, logit_scale, logit_bias,
    out_img, out_txt, out_wi, out_wt,
    w, x_in, proj, unit, norm, ours, other, coef_a, coef_b,
    a_own, a_part, a_out, a_mid, a_tot,
    b_own, b_part, b_out, b_mid, b_tot,
    y_out, y_in, back, perm_a, perm_b, feat_grad, feat_in,
    wa_own, wa_part, wa_out, wa_mid, wa_tot,
    wb_own, wb_part, wb_out, wb_mid, wb_tot,
    wa2_out, wa2_in, wb2_out, wb2_in, fin, y3_out, y3_in,
    load_sem, send_sem, recv_sem,
):
    blk = lax.axis_index("blk")
    rep = lax.axis_index("rep")
    z = blk // 8
    x = lax.rem(blk // 2, 4)
    y_hi = lax.rem(blk, 2)
    y_lo = rep // 2
    y = 2 * y_hi + y_lo
    core = lax.rem(rep, 2)

    def at(x_, y_, z_, core_):
        return {"blk": (z_ * 4 + x_) * 2 + y_ // 2, "rep": lax.rem(y_, 2) * 2 + core_}

    x_r, x_l, x_o = (at(wrap(x + d), y, z, core) for d in (1, -1, 2))
    z_r, z_l, z_o = (at(x, y, wrap(z + d), core) for d in (1, -1, 2))
    y_r, y_l, y_o = (at(x, wrap(y + d), z, core) for d in (1, -1, 2))
    sib = at(x, y, z, 1 - core)
    mate = {"blk": blk, "rep": lax.rem(rep + 2, 4)}
    a_r, a_l = (at(wrap(x + d * (1 - y_lo)), y, wrap(z + d * y_lo), core) for d in (1, -1))
    b_r, b_l = (at(wrap(x + d * y_lo), y, wrap(z + d * (1 - y_lo)), core) for d in (1, -1))

    barrier = pltpu.get_barrier_semaphore()
    for device in (x_r, x_l, x_o, z_r, z_l, z_o, y_r, y_l, y_o, sib):
        pl.semaphore_signal(barrier, inc=1, device_id=device, device_id_type=MESH)

    copies = Copies(send_sem, recv_sem)
    is_img = y_lo == 0
    is_txt = y_lo == 1

    parts = (pl.ds(0, DEEP), pl.ds(DEEP, D - DEEP))

    def load_own(feat, weight):
        return [pltpu.make_async_copy(feat, x_in.at[0], load_sem.at[0])] + [
            pltpu.make_async_copy(weight.at[p], w.at[0, p], load_sem.at[1 + k]) for k, p in enumerate(parts)
        ]

    load_img = load_own(img_feat, img_weight)
    load_txt = load_own(txt_feat, txt_weight)
    load_other = [pltpu.make_async_copy(img_feat, x_in.at[1], load_sem.at[3]),
                  pltpu.make_async_copy(img_weight, w.at[1], load_sem.at[4])]

    @pl.when(is_img)
    def _():
        for c in load_img:
            c.start()

    @pl.when(is_txt)
    def _():
        for c in (*load_txt, *load_other):
            c.start()

    own_lo = pl.ds(pl.multiple_of(core * HALF, HALF), HALF)
    own_hi = pl.ds(pl.multiple_of(ROWS + core * HALF, HALF), HALF)

    def own_rows(k):
        return jnp.concatenate([x_in[k, own_lo, :], x_in[k, own_hi, :]], axis=0)

    def normed():
        p = proj[...]
        n = jnp.sqrt(jnp.sum(p * p, axis=1, keepdims=True) + 1e-06)
        return n, p / n

    def rows_at(ref, slot, c, begin=0, size=ROWS):
        return ref.at[pl.ds(pl.multiple_of(slot * BLOCK + c * ROWS + begin, 16), size)]

    new = copies.new
    bit = ROWS // GIVE
    give = [
        new(rows_at(ours, OWN, core, q * bit, bit), rows_at(other, OWN, core, q * bit, bit), y_r)
        for q in range(GIVE)
    ]

    class RingGather:
        def __init__(self, ref, right, left, count):
            self.count, chunk = count, ROWS // count
            self.order = [q if k % 2 == 0 else count - 1 - q for q in range(count // 2) for k in range(2)]

            def of(slot, q):
                return rows_at(ref, slot, core, q * chunk, chunk)

            every = range(count)
            self.to_right = [new(of(OWN, q), of(LEFT, q), right) for q in every]
            self.to_left = [new(of(OWN, q), of(RIGHT, q), left) for q in every]
            self.onward = [
                new(of(LEFT, q), of(OPP, q), right) if q < count // 2
                else new(of(RIGHT, q), of(OPP, q), left)
                for q in every
            ]

        def send_first(self):
            self.to_right[0].start()
            self.to_left[1].start()

        def send_second(self):
            self.to_right[0].wait_send()
            self.to_right[1].start()
            self.to_left[1].wait_send()
            self.to_left[0].start()

        def forward(self, q):
            (self.to_right if q < self.count // 2 else self.to_left)[q].wait_recv()
            self.onward[q].start()

        def wait_near(self):
            for q in range(self.count):
                (self.to_left if q < self.count // 2 else self.to_right)[q].wait_recv()

        def wait_far(self):
            for c in self.onward:
                c.wait_recv()

        def wait_sent(self):
            for c in (self.to_right[1], self.to_left[0], *self.onward):
                c.wait_send()

    ga = RingGather(ours, a_r, a_l, GATHER)
    gb = RingGather(other, b_r, b_l, GIVE)
    share_a = [new(rows_at(ours, s, core), rows_at(ours, s, core), sib) for s in range(4)]
    share_b = [new(rows_at(other, s, core), rows_at(other, s, core), sib) for s in range(4)]

    load_img[0].wait()
    load_img[1].wait()
    first = own_rows(0)
    proj[...] = nn(first[:, :DEEP], w[0, :DEEP, :])
    load_img[2].wait()
    proj[...] = proj[...] + nn(first[:, DEEP:], w[0, DEEP:, :])
    n, u = normed()
    unit[...] = u
    norm[...] = jnp.broadcast_to(n, norm.shape)
    rows_at(ours, OWN, core)[...] = u.astype(BF16)

    pl.semaphore_wait(barrier, 10)

    ga.send_first()

    @pl.when(is_txt)
    def _():
        give[0].start()

    share_a[OWN].start()

    @pl.when(is_txt)
    def _():
        for c in load_other:
            c.wait()
        proj[...] = nn(own_rows(1), w[1])
        _, v = normed()
        rows_at(other, OWN, core)[...] = v.astype(BF16)
        gb.send_first()

    ga.send_second()

    @pl.when(is_txt)
    def _():
        give[0].wait_send()
        give[1].start()

    for q in range(GATHER):
        ga.forward(q)

    @pl.when(is_txt)
    def _():
        gb.send_second()

    @pl.when(is_img)
    def _():
        for q in range(GIVE):
            give[q].wait_recv()
            gb.to_right[q].start()
            gb.to_left[q].start()

    share_b[OWN].start()

    def permuted(out, x_first):
        def step(q, _):
            r = lax.broadcasted_iota(jnp.int32, (PART, 1), 0)
            zero = r * 0
            inner = zero
            for j in range(1, 4):
                inner = inner + jnp.where(r >= PIECE * j, 1, 0)
            k = r - PIECE * inner
            yy = zero
            for j in range(1, 4):
                yy = yy + jnp.where(k >= 9 * j, 1, 0)
            i = k - 9 * yy

            def offset(s):
                return s + jnp.where(s == 2, 1, 0) - jnp.where(s == 3, 1, 0)

            outer = zero + q
            x_s, z_s = (outer, inner) if x_first else (inner, outer)
            xx = jnp.bitwise_and(x + offset(x_s), 3)
            zz = jnp.bitwise_and(z + offset(z_s), 3)
            source = 72 * (4 * zz + xx) + 18 * yy + 9 * core + i
            column = lax.broadcasted_iota(jnp.int32, (PART, D), 1)
            chosen = jnp.where(column == source, 1.0, 0.0).astype(BF16)
            at_rows = pl.ds(pl.multiple_of(q * PART, 16), PART)
            out[at_rows, :] = nt(chosen, x_in[0]).astype(BF16)
            return 0

        lax.fori_loop(0, 4, step, 0)

    permuted(perm_a, True)
    ga.wait_near()
    share_a[LEFT].start()
    share_a[RIGHT].start()
    for q in gb.order:
        gb.forward(q)
    permuted(perm_b, False)
    ga.wait_far()
    share_a[OPP].start()

    half = 0.5 * logit_scale[0]
    half_bias = 0.5 * logit_bias[0]

    def coefs(out, rows_of, cols_of, first, count, s, slots):
        rows = jnp.concatenate([rows_at(rows_of, k, core)[...] for k in range(first, first + count)], axis=0)
        cols = pl.ds(s * BLOCK, slots * BLOCK)
        value = half * jnp.tanh(half * nt(rows, cols_of[cols, :]) + half_bias)
        if first == OWN and s == OWN:
            r = lax.broadcasted_iota(jnp.int32, value.shape, 0) + core * ROWS
            c = lax.broadcasted_iota(jnp.int32, value.shape, 1)
            r = jnp.where(r < (core + 1) * ROWS, r + (1 - y_lo) * 4 * BLOCK, 4 * BLOCK)
            value = jnp.where(r == c, value - half, value + half)
        else:
            value = value + half
        out[pl.ds(first * ROWS, count * ROWS), cols] = value.astype(BF16)

    near = (RIGHT, LEFT)
    share_b[OWN].wait_recv()
    coefs(coef_a, ours, other, 0, 4, OWN, 1)
    for c in share_a:
        c.wait_recv()
    coefs(coef_b, other, ours, OWN, 1, 0, 4)

    gb.wait_near()
    for k in near:
        share_b[k].start()
    coefs(coef_b, other, ours, RIGHT, 2, 0, 4)
    gb.wait_far()
    share_b[OPP].start()

    size = ROWS // PASSES
    blocks = [pl.ds(h * size, size) for h in range(PASSES)]
    ra = [RingSum(copies, a_r, a_l, a_out, a_part, a_mid, a_tot, h * size, size, size // 2) for h in range(PASSES)]
    rb = [RingSum(copies, b_r, b_l, b_out, b_part, b_mid, b_tot, h * size, size, size // 2) for h in range(PASSES)]

    coefs(coef_b, other, ours, OPP, 1, 0, 4)
    b_out[2] = nn(coef_b[OPP * ROWS:, :], ours[...]).astype(BF16)
    for ring in rb:
        ring.send_opposite()
    for k in (*near, OPP):
        share_b[k].wait_recv()
    coefs(coef_a, ours, other, 0, 4, RIGHT, 3)
    a_out[2] = nn(coef_a[OPP * ROWS:, :], other[...]).astype(BF16)
    for ring in ra:
        ring.send_opposite()
    both = nn(coef_b[ROWS:3 * ROWS, :], ours[...])
    b_part[0] = both[:ROWS]
    b_part[1] = both[ROWS:]
    rb[0].send_direct()
    both = nn(coef_a[ROWS:3 * ROWS, :], other[...])
    a_part[0] = both[:ROWS]
    a_part[1] = both[ROWS:]
    ra[0].send_direct()
    rb[0].send_summed()
    ra[0].send_summed()
    for h in range(1, PASSES):
        rb[h].send_direct()
        ra[h].send_direct()
    b_own[...] = nn(coef_b[:ROWS, :], ours[...])
    a_own[...] = nn(coef_a[:ROWS, :], other[...])
    for h in range(1, PASSES):
        rb[h].send_summed()
        ra[h].send_summed()

    hop = [new(y_out.at[b], y_in.at[b], y_l) for b in blocks]
    give_back = []
    for h, b in enumerate(blocks):
        y_out[b, :] = (b_own[b, :] + rb[h].received()).astype(BF16)
        hop[h].start()
        proj[b, :] = a_own[b, :] + ra[h].received()

    for h, b in enumerate(blocks):
        hop[h].wait_recv()
        direction = proj[b, :] + y_in[b, :].astype(F32)
        u_own = unit[b, :]
        along = jnp.sum(u_own * direction, axis=1, keepdims=True)
        mine = ((direction - u_own * along) / norm[b, :1]).astype(BF16)
        begin = h * size
        where = pl.ds(pl.multiple_of((begin // HALF) * ROWS + core * HALF + begin % HALF, 32), size)
        back[where, :] = mine
        c = new(back.at[where], back.at[where], sib)
        c.start()
        give_back.append(c)
    for c in give_back:
        c.wait_recv()

    wa = RingSum(copies, x_r, x_l, wa_out, wa_part, wa_mid, wa_tot, 0, PART, CUT)
    wb = RingSum(copies, z_r, z_l, wb_out, wb_part, wb_mid, wb_tot, 0, PART, CUT)

    def part_a(s):
        return nn(perm_a[s * PART:(s + 1) * PART, :], back[:, :COLS_A])

    def part_b(s):
        return nn(perm_b[s * PART:(s + 1) * PART, :], back[:, COLS_A:])

    wa_out[2] = part_a(OPP).astype(BF16)
    wa.send_opposite()
    wb_out[2] = part_b(OPP).astype(BF16)
    wb.send_opposite()
    wa_part[0] = part_a(RIGHT)
    wa_part[1] = part_a(LEFT)
    wa.send_direct()
    wb_part[0] = part_b(RIGHT)
    wb_part[1] = part_b(LEFT)
    wb.send_direct()
    wa_own[:PART, :] = part_a(OWN)
    wb_own[:PART, :] = part_b(OWN)
    wa_own[PART:, :] = jnp.zeros((16, COLS_A), F32)
    wb_own[PART:, :] = jnp.zeros((16, COLS_B), F32)
    wa.send_summed()
    wb.send_summed()

    grad = nt(jnp.concatenate([back[own_lo, :], back[own_hi, :]], axis=0), w[0]).astype(BF16)
    feat_grad[0] = grad[:HALF]
    feat_grad[1] = grad[HALF:]
    give_grad = new(feat_grad.at[1 - y_lo], feat_in, mate)
    give_grad.start()

    wa_own[:PART, :] = wa_own[:PART, :] + wa.received()

    def second(own, out, inbox, right, left, opposite):
        sends = []
        for s, there, device in ((OPP, OPP, opposite), (RIGHT, LEFT, right), (LEFT, RIGHT, left)):
            out[s] = own[s * PIECE:s * PIECE + 48, :].astype(BF16)
            c = new(out.at[s], inbox.at[there], device)
            c.start()
            sends.append(c)
        return sends

    sa = second(wa_own, wa2_out, wa2_in, z_r, z_l, z_o)
    wb_own[:PART, :] = wb_own[:PART, :] + wb.received()
    sb = second(wb_own, wb2_out, wb2_in, x_r, x_l, x_o)

    for c in sa:
        c.wait_recv()
    fin[:, :COLS_A] = (
        wa_own[:48, :] + wa2_in[1].astype(F32) + wa2_in[2].astype(F32) + wa2_in[3].astype(F32)
    )
    for c in sb:
        c.wait_recv()
    fin[:, COLS_A:] = (
        wb_own[:48, :] + wb2_in[1].astype(F32) + wb2_in[2].astype(F32) + wb2_in[3].astype(F32)
    )

    for j in range(4):
        y3_out[j] = fin[9 * j:9 * j + 16, :].astype(BF16)
    s3 = []
    for d, device in ((2, y_o), (1, y_r), (3, y_l)):
        c = new(y3_out.at[wrap(y + d)], y3_in.at[y], device)
        c.start()
        s3.append(c)
    y3_in[y] = y3_out[y]

    give_grad.wait_recv()

    @pl.when(is_img)
    def _():
        out_img[...] = feat_grad[0]
        out_txt[...] = feat_in[...]

    @pl.when(is_txt)
    def _():
        out_img[...] = feat_in[...]
        out_txt[...] = feat_grad[1]

    for c in s3:
        c.wait_recv()
    out_wi[...] = (y3_in[0].astype(F32) + y3_in[2].astype(F32))[:9]
    out_wt[...] = (y3_in[1].astype(F32) + y3_in[3].astype(F32))[:9]

    @pl.when(is_txt)
    def _():
        give[1].wait_send()

    @pl.when(is_img)
    def _():
        gb.to_right[0].wait_send()
        gb.to_left[1].wait_send()

    for c in (*share_a, *share_b, *hop, *give_back, give_grad, *sa, *sb, *s3):
        c.wait_send()
    for ring in (ga, gb, *ra, *rb, wa, wb):
        ring.wait_sent()


def hand_out(a, b, c, d, out_a, out_b, out_c, out_d):
    for src, dst in ((a, out_a), (b, out_b), (c, out_c), (d, out_d)):
        dst[...] = src[...]


def ring_scratch(rows, cols):
    return [
        pltpu.VMEM((3, rows, cols), BF16),
        pltpu.VMEM((rows, cols), BF16),
        pltpu.VMEM((2, rows, cols), BF16),
    ]


N_COPIES = 112


def per_device(img_feat, txt_feat, img_weight, txt_weight, logit_scale, logit_bias):
    anywhere = pl.BlockSpec(memory_space=pl.ANY)
    vmem = pl.BlockSpec(memory_space=pltpu.VMEM)
    V = pltpu.VMEM
    outs = pl.pallas_call(
        kernel,
        name="pair_gradients",
        out_shape=(
            pltpu.VMEM((HALF, D), BF16),
            pltpu.VMEM((HALF, D), BF16),
            pltpu.VMEM((9, D), F32),
            pltpu.VMEM((9, D), F32),
        ),
        in_specs=[anywhere] * 4 + [pl.BlockSpec(memory_space=pltpu.SMEM)] * 2,
        out_specs=(vmem,) * 4,
        scratch_shapes=[
            V((2, D, D), BF16),
            V((2, BLOCK, D), BF16),
            V((ROWS, D), F32),
            V((ROWS, D), F32),
            V((ROWS, 128), F32),
            V((4 * BLOCK, D), BF16),
            V((4 * BLOCK, D), BF16),
            V((4 * ROWS, 4 * BLOCK), BF16),
            V((4 * ROWS, 4 * BLOCK), BF16),
            V((ROWS, D), F32),
            V((2, ROWS, D), F32),
            *ring_scratch(ROWS, D),
            V((ROWS, D), F32),
            V((2, ROWS, D), F32),
            *ring_scratch(ROWS, D),
            V((ROWS, D), BF16),
            V((ROWS, D), BF16),
            V((BLOCK, D), BF16),
            V((4 * PART, BLOCK), BF16),
            V((4 * PART, BLOCK), BF16),
            V((2, HALF, D), BF16),
            V((HALF, D), BF16),
            V((PART + 16, COLS_A), F32),
            V((2, PART, COLS_A), F32),
            *ring_scratch(PART, COLS_A),
            V((PART + 16, COLS_B), F32),
            V((2, PART, COLS_B), F32),
            *ring_scratch(PART, COLS_B),
            V((4, 48, COLS_A), BF16),
            V((4, 48, COLS_A), BF16),
            V((4, 48, COLS_B), BF16),
            V((4, 48, COLS_B), BF16),
            V((48, D), F32),
            V((4, 16, D), BF16),
            V((4, 16, D), BF16),
            pltpu.SemaphoreType.DMA((5,)),
            pltpu.SemaphoreType.DMA((N_COPIES,)),
            pltpu.SemaphoreType.DMA((N_COPIES,)),
        ],
        compiler_params=pltpu.CompilerParams(
            collective_id=0, has_side_effects=True, vmem_limit_bytes=60 * 1024 * 1024
        ),
        cost_estimate=pl.CostEstimate(
            flops=6_000_000_000, bytes_accessed=8_000_000, transcendentals=600_000
        ),
    )(
        img_feat, txt_feat, img_weight, txt_weight,
        logit_scale, logit_bias,
    )
    return pl.pallas_call(
        hand_out,
        name="hand_out",
        out_shape=tuple(jax.ShapeDtypeStruct(o.shape, o.dtype) for o in outs),
        in_specs=[vmem] * 4,
        out_specs=(vmem,) * 4,
        compiler_params=pltpu.CompilerParams(vmem_limit_bytes=4 * 1024 * 1024),
    )(*outs)


def solution(mesh):
    placed = (P("blk", None), P("blk", None), P(), P(), P(), P())
    return jax.shard_map(
        per_device,
        mesh=mesh,
        in_specs=placed,
        out_specs=(P(("blk", "rep"), None),) * 4,
        check_vma=False,
    )
```

```python
import jax
import jax.numpy as jnp
from jax import lax
from jax.experimental import pallas as pl
from jax.experimental.pallas import tpu as pltpu
from jax.sharding import PartitionSpec as P

MESH = pl.DeviceIdType.MESH
F32 = jnp.float32
BF16 = jnp.bfloat16
D = 1152
BLOCK = 256
ROWS = 128
HALF = 64
OWN, RIGHT, LEFT, OPP = 0, 1, 2, 3
PART = 144
PIECE = 36
CUT = 80
COLS_A = 640
COLS_B = D - COLS_A
DEEP = 512
GIVE = 2
GATHER = 2
PASSES = 2


def nt(a, b):
    return lax.dot_general(a, b, (((1,), (1,)), ((), ())), preferred_element_type=F32)


def nn(a, b):
    return jnp.dot(a, b, preferred_element_type=F32)


def wrap(v):
    return lax.rem(v + 4, 4)


class Copies:
    def __init__(self, send, recv):
        self.send, self.recv, self.count = send, recv, 0

    def new(self, src, dst, device):
        k = self.count
        self.count += 1
        return pltpu.make_async_remote_copy(
            src_ref=src, dst_ref=dst, send_sem=self.send.at[k], recv_sem=self.recv.at[k],
            device_id=device, device_id_type=MESH,
        )


class RingSum:
    def __init__(self, copies, right, left, out, part, mid, total, start, rows, cut):
        self.out, self.part, self.mid, self.total = out, part, mid, total
        lo, hi = pl.ds(start, cut), pl.ds(start + cut, rows - cut)
        self.lo, self.hi, self.rows = lo, hi, pl.ds(start, rows)
        new = copies.new
        self.opp_r = new(out.at[2, lo], mid.at[lo], right)
        self.opp_l = new(out.at[2, hi], mid.at[hi], left)
        self.right_hi = new(out.at[0, hi], total.at[0, hi], right)
        self.left_lo = new(out.at[1, lo], total.at[1, lo], left)
        self.right_lo = new(out.at[0, lo], total.at[0, lo], right)
        self.left_hi = new(out.at[1, hi], total.at[1, hi], left)

    def send_opposite(self):
        self.opp_r.start()
        self.opp_l.start()

    def send_direct(self):
        self.out[0, self.hi, :] = self.part[0, self.hi, :].astype(BF16)
        self.right_hi.start()
        self.out[1, self.lo, :] = self.part[1, self.lo, :].astype(BF16)
        self.left_lo.start()

    def send_summed(self):
        self.opp_r.wait_recv()
        self.out[0, self.lo, :] = (
            self.part[0, self.lo, :] + self.mid[self.lo, :].astype(F32)
        ).astype(BF16)
        self.right_lo.start()
        self.opp_l.wait_recv()
        self.out[1, self.hi, :] = (
            self.part[1, self.hi, :] + self.mid[self.hi, :].astype(F32)
        ).astype(BF16)
        self.left_hi.start()

    def received(self):
        self.left_lo.wait_recv()
        self.right_hi.wait_recv()
        self.right_lo.wait_recv()
        self.left_hi.wait_recv()
        return self.total[0, self.rows, :].astype(F32) + self.total[1, self.rows, :].astype(F32)

    def wait_sent(self):
        for c in (self.opp_r, self.opp_l, self.right_hi, self.left_lo, self.right_lo, self.left_hi):
            c.wait_send()


def kernel(
    img_feat, txt_feat, img_weight, txt_weight, logit_scale, logit_bias,
    out_img, out_txt, out_wi, out_wt,
    w, x_in, proj, unit, norm, ours, other, coef_a, coef_b,
    a_own, a_part, a_out, a_mid, a_tot,
    b_own, b_part, b_out, b_mid, b_tot,
    y_out, y_in, back, perm_a, perm_b, feat_grad, feat_in,
    wa_own, wa_part, wa_out, wa_mid, wa_tot,
    wb_own, wb_part, wb_out, wb_mid, wb_tot,
    wa2_out, wa2_in, wb2_out, wb2_in, fin, y3_out, y3_in,
    load_sem, send_sem, recv_sem,
):
    blk = lax.axis_index("blk")
    rep = lax.axis_index("rep")
    z = blk // 8
    x = lax.rem(blk // 2, 4)
    y_hi = lax.rem(blk, 2)
    y_lo = rep // 2
    y = 2 * y_hi + y_lo
    core = lax.rem(rep, 2)

    def at(x_, y_, z_, core_):
        return {"blk": (z_ * 4 + x_) * 2 + y_ // 2, "rep": lax.rem(y_, 2) * 2 + core_}

    x_r, x_l, x_o = (at(wrap(x + d), y, z, core) for d in (1, -1, 2))
    z_r, z_l, z_o = (at(x, y, wrap(z + d), core) for d in (1, -1, 2))
    y_r, y_l, y_o = (at(x, wrap(y + d), z, core) for d in (1, -1, 2))
    sib = at(x, y, z, 1 - core)
    mate = {"blk": blk, "rep": lax.rem(rep + 2, 4)}
    a_r, a_l = (at(wrap(x + d * (1 - y_lo)), y, wrap(z + d * y_lo), core) for d in (1, -1))
    b_r, b_l = (at(wrap(x + d * y_lo), y, wrap(z + d * (1 - y_lo)), core) for d in (1, -1))

    barrier = pltpu.get_barrier_semaphore()
    for device in (x_r, x_l, x_o, z_r, z_l, z_o, y_r, y_l, y_o, sib):
        pl.semaphore_signal(barrier, inc=1, device_id=device, device_id_type=MESH)

    copies = Copies(send_sem, recv_sem)
    is_img = y_lo == 0
    is_txt = y_lo == 1

    parts = (pl.ds(0, DEEP), pl.ds(DEEP, D - DEEP))

    def load_own(feat, weight):
        return [pltpu.make_async_copy(feat, x_in.at[0], load_sem.at[0])] + [
            pltpu.make_async_copy(weight.at[p], w.at[0, p], load_sem.at[1 + k]) for k, p in enumerate(parts)
        ]

    load_img = load_own(img_feat, img_weight)
    load_txt = load_own(txt_feat, txt_weight)
    load_other = [pltpu.make_async_copy(img_feat, x_in.at[1], load_sem.at[3]),
                  pltpu.make_async_copy(img_weight, w.at[1], load_sem.at[4])]

    @pl.when(is_img)
    def _():
        for c in load_img:
            c.start()

    @pl.when(is_txt)
    def _():
        for c in (*load_txt, *load_other):
            c.start()

    own_lo = pl.ds(pl.multiple_of(core * HALF, HALF), HALF)
    own_hi = pl.ds(pl.multiple_of(ROWS + core * HALF, HALF), HALF)

    def own_rows(k):
        return jnp.concatenate([x_in[k, own_lo, :], x_in[k, own_hi, :]], axis=0)

    def normed():
        p = proj[...]
        n = jnp.sqrt(jnp.sum(p * p, axis=1, keepdims=True) + 1e-06)
        return n, p / n

    def rows_at(ref, slot, c, begin=0, size=ROWS):
        return ref.at[pl.ds(pl.multiple_of(slot * BLOCK + c * ROWS + begin, 16), size)]

    new = copies.new
    bit = ROWS // GIVE
    give = [
        new(rows_at(ours, OWN, core, q * bit, bit), rows_at(other, OWN, core, q * bit, bit), y_r)
        for q in range(GIVE)
    ]

    class RingGather:
        def __init__(self, ref, right, left, count):
            self.count, chunk = count, ROWS // count
            self.order = [q if k % 2 == 0 else count - 1 - q for q in range(count // 2) for k in range(2)]

            def of(slot, q):
                return rows_at(ref, slot, core, q * chunk, chunk)

            every = range(count)
            self.to_right = [new(of(OWN, q), of(LEFT, q), right) for q in every]
            self.to_left = [new(of(OWN, q), of(RIGHT, q), left) for q in every]
            self.onward = [
                new(of(LEFT, q), of(OPP, q), right) if q < count // 2
                else new(of(RIGHT, q), of(OPP, q), left)
                for q in every
            ]

        def send_first(self):
            self.to_right[0].start()
            self.to_left[1].start()

        def send_second(self):
            self.to_right[0].wait_send()
            self.to_right[1].start()
            self.to_left[1].wait_send()
            self.to_left[0].start()

        def forward(self, q):
            (self.to_right if q < self.count // 2 else self.to_left)[q].wait_recv()
            self.onward[q].start()

        def wait_near(self):
            for q in range(self.count):
                (self.to_left if q < self.count // 2 else self.to_right)[q].wait_recv()

        def wait_far(self):
            for c in self.onward:
                c.wait_recv()

        def wait_sent(self):
            for c in (self.to_right[1], self.to_left[0], *self.onward):
                c.wait_send()

    ga = RingGather(ours, a_r, a_l, GATHER)
    gb = RingGather(other, b_r, b_l, GIVE)
    share_a = [new(rows_at(ours, s, core), rows_at(ours, s, core), sib) for s in range(4)]
    share_b = [new(rows_at(other, s, core), rows_at(other, s, core), sib) for s in range(4)]

    load_img[0].wait()
    load_img[1].wait()
    first = own_rows(0)
    proj[...] = nn(first[:, :DEEP], w[0, :DEEP, :])
    load_img[2].wait()
    proj[...] = proj[...] + nn(first[:, DEEP:], w[0, DEEP:, :])
    n, u = normed()
    unit[...] = u
    norm[...] = jnp.broadcast_to(n, norm.shape)
    rows_at(ours, OWN, core)[...] = u.astype(BF16)

    pl.semaphore_wait(barrier, 10)

    ga.send_first()

    @pl.when(is_txt)
    def _():
        give[0].start()

    share_a[OWN].start()

    @pl.when(is_txt)
    def _():
        for c in load_other:
            c.wait()
        proj[...] = nn(own_rows(1), w[1])
        _, v = normed()
        rows_at(other, OWN, core)[...] = v.astype(BF16)
        gb.send_first()

    ga.send_second()

    @pl.when(is_txt)
    def _():
        give[0].wait_send()
        give[1].start()

    for q in range(GATHER):
        ga.forward(q)

    @pl.when(is_txt)
    def _():
        gb.send_second()

    @pl.when(is_img)
    def _():
        for q in range(GIVE):
            give[q].wait_recv()
            gb.to_right[q].start()
            gb.to_left[q].start()

    share_b[OWN].start()

    def permuted(out, x_first):
        def step(q, _):
            r = lax.broadcasted_iota(jnp.int32, (PART, 1), 0)
            zero = r * 0
            inner = zero
            for j in range(1, 4):
                inner = inner + jnp.where(r >= PIECE * j, 1, 0)
            k = r - PIECE * inner
            yy = zero
            for j in range(1, 4):
                yy = yy + jnp.where(k >= 9 * j, 1, 0)
            i = k - 9 * yy

            def offset(s):
                return s + jnp.where(s == 2, 1, 0) - jnp.where(s == 3, 1, 0)

            outer = zero + q
            x_s, z_s = (outer, inner) if x_first else (inner, outer)
            xx = jnp.bitwise_and(x + offset(x_s), 3)
            zz = jnp.bitwise_and(z + offset(z_s), 3)
            source = 72 * (4 * zz + xx) + 18 * yy + 9 * core + i
            column = lax.broadcasted_iota(jnp.int32, (PART, D), 1)
            chosen = jnp.where(column == source, 1.0, 0.0).astype(BF16)
            at_rows = pl.ds(pl.multiple_of(q * PART, 16), PART)
            out[at_rows, :] = nt(chosen, x_in[0]).astype(BF16)
            return 0

        lax.fori_loop(0, 4, step, 0)

    ga.wait_near()
    share_a[LEFT].start()
    share_a[RIGHT].start()
    permuted(perm_a, True)
    for q in gb.order:
        gb.forward(q)
    permuted(perm_b, False)
    ga.wait_far()
    share_a[OPP].start()

    half = 0.5 * logit_scale[0]
    half_bias = 0.5 * logit_bias[0]

    def coefs(out, rows_of, cols_of, first, count, s, slots):
        rows = jnp.concatenate([rows_at(rows_of, k, core)[...] for k in range(first, first + count)], axis=0)
        cols = pl.ds(s * BLOCK, slots * BLOCK)
        value = half * jnp.tanh(half * nt(rows, cols_of[cols, :]) + half_bias)
        if first == OWN and s == OWN:
            r = lax.broadcasted_iota(jnp.int32, value.shape, 0) + core * ROWS
            c = lax.broadcasted_iota(jnp.int32, value.shape, 1)
            r = jnp.where(r < (core + 1) * ROWS, r + (1 - y_lo) * 4 * BLOCK, 4 * BLOCK)
            value = jnp.where(r == c, value - half, value + half)
        else:
            value = value + half
        out[pl.ds(first * ROWS, count * ROWS), cols] = value.astype(BF16)

    near = (RIGHT, LEFT)
    share_b[OWN].wait_recv()
    coefs(coef_a, ours, other, 0, 4, OWN, 1)
    for c in share_a:
        c.wait_recv()
    coefs(coef_b, other, ours, OWN, 1, 0, 4)

    gb.wait_near()
    for k in near:
        share_b[k].start()
    coefs(coef_b, other, ours, RIGHT, 2, 0, 4)
    gb.wait_far()
    share_b[OPP].start()

    size = ROWS // PASSES
    blocks = [pl.ds(h * size, size) for h in range(PASSES)]
    ra = [RingSum(copies, a_r, a_l, a_out, a_part, a_mid, a_tot, h * size, size, size // 2) for h in range(PASSES)]
    rb = [RingSum(copies, b_r, b_l, b_out, b_part, b_mid, b_tot, h * size, size, size // 2) for h in range(PASSES)]

    coefs(coef_b, other, ours, OPP, 1, 0, 4)
    b_out[2] = nn(coef_b[OPP * ROWS:, :], ours[...]).astype(BF16)
    for ring in rb:
        ring.send_opposite()
    for k in (*near, OPP):
        share_b[k].wait_recv()
    coefs(coef_a, ours, other, 0, 4, RIGHT, 3)
    a_out[2] = nn(coef_a[OPP * ROWS:, :], other[...]).astype(BF16)
    ra[0].send_opposite()
    both = nn(coef_b[ROWS:3 * ROWS, :], ours[...])
    for ring in ra[1:]:
        ring.send_opposite()
    b_part[0] = both[:ROWS]
    b_part[1] = both[ROWS:]
    rb[0].send_direct()
    both = nn(coef_a[ROWS:3 * ROWS, :], other[...])
    a_part[0] = both[:ROWS]
    a_part[1] = both[ROWS:]
    ra[0].send_direct()
    rb[0].send_summed()
    ra[0].send_summed()
    for h in range(1, PASSES):
        rb[h].send_direct()
        ra[h].send_direct()
    b_own[...] = nn(coef_b[:ROWS, :], ours[...])
    a_own[...] = nn(coef_a[:ROWS, :], other[...])
    for h in range(1, PASSES):
        rb[h].send_summed()
        ra[h].send_summed()

    hop = [new(y_out.at[b], y_in.at[b], y_l) for b in blocks]
    give_back = []
    for h, b in enumerate(blocks):
        y_out[b, :] = (b_own[b, :] + rb[h].received()).astype(BF16)
        hop[h].start()

    for h, b in enumerate(blocks):
        proj[b, :] = a_own[b, :] + ra[h].received()

    for h, b in enumerate(blocks):
        hop[h].wait_recv()
        direction = proj[b, :] + y_in[b, :].astype(F32)
        u_own = unit[b, :]
        along = jnp.sum(u_own * direction, axis=1, keepdims=True)
        mine = ((direction - u_own * along) / norm[b, :1]).astype(BF16)
        begin = h * size
        where = pl.ds(pl.multiple_of((begin // HALF) * ROWS + core * HALF + begin % HALF, 32), size)
        back[where, :] = mine
        c = new(back.at[where], back.at[where], sib)
        c.start()
        give_back.append(c)
    for c in give_back:
        c.wait_recv()

    wa = RingSum(copies, x_r, x_l, wa_out, wa_part, wa_mid, wa_tot, 0, PART, CUT)
    wb = RingSum(copies, z_r, z_l, wb_out, wb_part, wb_mid, wb_tot, 0, PART, CUT)

    def part_a(s):
        return nn(perm_a[s * PART:(s + 1) * PART, :], back[:, :COLS_A])

    def part_b(s):
        return nn(perm_b[s * PART:(s + 1) * PART, :], back[:, COLS_A:])

    wa_out[2] = part_a(OPP).astype(BF16)
    wa.send_opposite()
    wb_out[2] = part_b(OPP).astype(BF16)
    wb.send_opposite()
    wa_part[0] = part_a(RIGHT)
    wa_part[1] = part_a(LEFT)
    wa.send_direct()
    wb_part[0] = part_b(RIGHT)
    wb_part[1] = part_b(LEFT)
    wb.send_direct()
    wa_own[:PART, :] = part_a(OWN)
    wb_own[:PART, :] = part_b(OWN)
    wa_own[PART:, :] = jnp.zeros((16, COLS_A), F32)
    wb_own[PART:, :] = jnp.zeros((16, COLS_B), F32)
    wa.send_summed()
    wb.send_summed()

    grad = nt(jnp.concatenate([back[own_lo, :], back[own_hi, :]], axis=0), w[0]).astype(BF16)
    feat_grad[0] = grad[:HALF]
    feat_grad[1] = grad[HALF:]
    give_grad = new(feat_grad.at[1 - y_lo], feat_in, mate)
    give_grad.start()

    wa_own[:PART, :] = wa_own[:PART, :] + wa.received()

    def second(own, out, inbox, right, left, opposite):
        sends = []
        for s, there, device in ((OPP, OPP, opposite), (RIGHT, LEFT, right), (LEFT, RIGHT, left)):
            out[s] = own[s * PIECE:s * PIECE + 48, :].astype(BF16)
            c = new(out.at[s], inbox.at[there], device)
            c.start()
            sends.append(c)
        return sends

    sa = second(wa_own, wa2_out, wa2_in, z_r, z_l, z_o)
    wb_own[:PART, :] = wb_own[:PART, :] + wb.received()
    sb = second(wb_own, wb2_out, wb2_in, x_r, x_l, x_o)

    for c in sa:
        c.wait_recv()
    fin[:, :COLS_A] = (
        wa_own[:48, :] + wa2_in[1].astype(F32) + wa2_in[2].astype(F32) + wa2_in[3].astype(F32)
    )
    for c in sb:
        c.wait_recv()
    fin[:, COLS_A:] = (
        wb_own[:48, :] + wb2_in[1].astype(F32) + wb2_in[2].astype(F32) + wb2_in[3].astype(F32)
    )

    for j in range(4):
        y3_out[j] = fin[9 * j:9 * j + 16, :].astype(BF16)
    s3 = []
    for d, device in ((2, y_o), (1, y_r), (3, y_l)):
        c = new(y3_out.at[wrap(y + d)], y3_in.at[y], device)
        c.start()
        s3.append(c)
    y3_in[y] = y3_out[y]

    give_grad.wait_recv()

    @pl.when(is_img)
    def _():
        out_img[...] = feat_grad[0]
        out_txt[...] = feat_in[...]

    @pl.when(is_txt)
    def _():
        out_img[...] = feat_in[...]
        out_txt[...] = feat_grad[1]

    for c in s3:
        c.wait_recv()
    out_wi[...] = (y3_in[0].astype(F32) + y3_in[2].astype(F32))[:9]
    out_wt[...] = (y3_in[1].astype(F32) + y3_in[3].astype(F32))[:9]

    @pl.when(is_txt)
    def _():
        give[1].wait_send()

    @pl.when(is_img)
    def _():
        gb.to_right[0].wait_send()
        gb.to_left[1].wait_send()

    for c in (*share_a, *share_b, *hop, *give_back, give_grad, *sa, *sb, *s3):
        c.wait_send()
    for ring in (ga, gb, *ra, *rb, wa, wb):
        ring.wait_sent()


def hand_out(a, b, c, d, out_a, out_b, out_c, out_d):
    for src, dst in ((a, out_a), (b, out_b), (c, out_c), (d, out_d)):
        dst[...] = src[...]


def ring_scratch(rows, cols):
    return [
        pltpu.VMEM((3, rows, cols), BF16),
        pltpu.VMEM((rows, cols), BF16),
        pltpu.VMEM((2, rows, cols), BF16),
    ]


N_COPIES = 112


def per_device(img_feat, txt_feat, img_weight, txt_weight, logit_scale, logit_bias):
    anywhere = pl.BlockSpec(memory_space=pl.ANY)
    vmem = pl.BlockSpec(memory_space=pltpu.VMEM)
    V = pltpu.VMEM
    outs = pl.pallas_call(
        kernel,
        name="pair_gradients",
        out_shape=(
            pltpu.VMEM((HALF, D), BF16),
            pltpu.VMEM((HALF, D), BF16),
            pltpu.VMEM((9, D), F32),
            pltpu.VMEM((9, D), F32),
        ),
        in_specs=[anywhere] * 4 + [pl.BlockSpec(memory_space=pltpu.SMEM)] * 2,
        out_specs=(vmem,) * 4,
        scratch_shapes=[
            V((2, D, D), BF16),
            V((2, BLOCK, D), BF16),
            V((ROWS, D), F32),
            V((ROWS, D), F32),
            V((ROWS, 128), F32),
            V((4 * BLOCK, D), BF16),
            V((4 * BLOCK, D), BF16),
            V((4 * ROWS, 4 * BLOCK), BF16),
            V((4 * ROWS, 4 * BLOCK), BF16),
            V((ROWS, D), F32),
            V((2, ROWS, D), F32),
            *ring_scratch(ROWS, D),
            V((ROWS, D), F32),
            V((2, ROWS, D), F32),
            *ring_scratch(ROWS, D),
            V((ROWS, D), BF16),
            V((ROWS, D), BF16),
            V((BLOCK, D), BF16),
            V((4 * PART, BLOCK), BF16),
            V((4 * PART, BLOCK), BF16),
            V((2, HALF, D), BF16),
            V((HALF, D), BF16),
            V((PART + 16, COLS_A), F32),
            V((2, PART, COLS_A), F32),
            *ring_scratch(PART, COLS_A),
            V((PART + 16, COLS_B), F32),
            V((2, PART, COLS_B), F32),
            *ring_scratch(PART, COLS_B),
            V((4, 48, COLS_A), BF16),
            V((4, 48, COLS_A), BF16),
            V((4, 48, COLS_B), BF16),
            V((4, 48, COLS_B), BF16),
            V((48, D), F32),
            V((4, 16, D), BF16),
            V((4, 16, D), BF16),
            pltpu.SemaphoreType.DMA((5,)),
            pltpu.SemaphoreType.DMA((N_COPIES,)),
            pltpu.SemaphoreType.DMA((N_COPIES,)),
        ],
        compiler_params=pltpu.CompilerParams(
            collective_id=0, has_side_effects=True, vmem_limit_bytes=60 * 1024 * 1024
        ),
        cost_estimate=pl.CostEstimate(
            flops=6_000_000_000, bytes_accessed=8_000_000, transcendentals=600_000
        ),
    )(
        img_feat, txt_feat, img_weight, txt_weight,
        logit_scale, logit_bias,
    )
    return pl.pallas_call(
        hand_out,
        name="hand_out",
        out_shape=tuple(jax.ShapeDtypeStruct(o.shape, o.dtype) for o in outs),
        in_specs=[vmem] * 4,
        out_specs=(vmem,) * 4,
        compiler_params=pltpu.CompilerParams(vmem_limit_bytes=4 * 1024 * 1024),
    )(*outs)


def solution(mesh):
    placed = (P("blk", None), P("blk", None), P(), P(), P(), P())
    return jax.shard_map(
        per_device,
        mesh=mesh,
        in_specs=placed,
        out_specs=(P(("blk", "rep"), None),) * 4,
        check_vma=False,
    )
```
